512 devices in a mesh: row: 16 (over z_lo, core), col: 8 (over z_hi, y), depth: 4 (over x).
Axes of the slice: x: 4, y: 4, z: 16 (z_hi: 2, z_lo: 8; z = z_hi * 8 + z_lo), core: 2. Of those that a mesh axis runs over, the one named last changes fastest.
Arguments:
- amplitudes: bfloat16 [8192, 256], P(('col', 'depth'), 'row'), may hold values from -6 to 6
- integrals: bfloat16 [16384, 256], P(('row', 'col'), 'depth'), may hold values from -0.375 to 0.375
- old_residual: float32 [8192, 16384], P(('col', 'depth'), 'row'), may hold values from -6 to 6
Outputs:
- new_residual: float32 [8192, 16384], P(('col', 'depth'), 'row')
The draws below stay inside these ranges and needn't reach their ends.
All inputs are finite; a program needn't handle non-finite values.
Results may differ from the reference program's by a relative error of at most 0.0003.
Values may be sent and summed in bfloat16 or wider, within the bound.
No kernel may reach another device: no remote copies, remote signals or barrier semaphores. Data moves between devices by JAX's collectives and lax.ppermute only.
A program may use at most 64 MiB of HBM per device.

```python
import jax
import jax.numpy as jnp
from jax import lax

CD = 256
NP = 8192
NAB = 16384


def block_scale(rng, extent, cuts, smallest, top_value):
    def one(dim, blocks):
        draws = jax.random.uniform(jax.random.fold_in(jax.random.fold_in(rng, 6), dim), (blocks,), jnp.float32, smallest / len(cuts), top_value / len(cuts))
        return jnp.repeat(jnp.exp(draws), extent[dim] // blocks).reshape((-1,) + (1,) * (len(extent) - dim - 1))

    factor_of = one(*cuts[0])
    for cut in cuts[1:]:
        factor_of = factor_of * one(*cut)
    return factor_of


def normal_values(rng, dims, spread, reach, split=(), held_as=jnp.bfloat16):
    array = jax.random.normal(rng, dims, jnp.float32) * spread
    if len(split) > 0:
        array = block_scale(rng, dims, split, -0.22, 0.18) * array
    return jnp.clip(array, min=-reach, max=reach).astype(held_as)


def setup_inputs(seed: int = 0) -> dict:
    splits = jax.random.split(jax.random.key(seed), 4)
    return {
        "amplitudes": normal_values(splits[0], (NP, CD), 1.0, 6.0, ((0, 32), (1, 16))),
        "integrals": normal_values(splits[1], (NAB, CD), CD ** -0.5, 0.375, ((0, 128), (1, 4))),
        "old_residual": normal_values(splits[2], (NP, NAB), 1.0, 6.0, ((0, 32), (1, 16)), jnp.float32),
    }


def reference(amplitudes, integrals, old_residual):
    ladder = lax.dot_general(amplitudes, integrals, (((1,), (1,)), ((), ())), preferred_element_type=jnp.float32)
    return old_residual + ladder
```

```python
import jax
import jax.numpy as jnp
from jax import lax
from jax.experimental import pallas as pl
from jax.experimental.pallas import tpu as pltpu
from jax.sharding import Mesh, PartitionSpec as P

Z_LO, CORES, Z_HI, Y, X = 8, 2, 2, 4, 4
ROW = ("z_lo", "core")
COL = ("z_hi", "y")
PLANE = ("y", "x")


def spread(block, axes, count):
    return lax.all_to_all(jnp.broadcast_to(block[None], (count,) + block.shape), axes, 0, 0)


def ladder_kernel(amp_ref, int_ref, old_ref, new_ref, held, sems):
    rows, width = held.shape[1:]
    amp = amp_ref[...].reshape(-1, rows)
    copies = []
    for part in range(held.shape[0]):
        half, pair = divmod(part, Y // 2)
        panels = []
        for y in (2 * pair, 2 * pair + 1):
            panel = int_ref[y * X:(y + 1) * X, half]
            panels.append(panel.reshape(-1, panel.shape[-1]))
        product = lax.dot_general(
            amp,
            jnp.concatenate(panels, axis=1),
            (((0,), (0,)), ((), ())),
            preferred_element_type=jnp.float32,
        )
        columns = pl.ds(part * width, width)
        held[part] = old_ref[:, columns] + product
        copy = pltpu.make_async_copy(held.at[part], new_ref.at[:, columns], sems.at[part])
        copy.start()
        copies.append(copy)
    for copy in copies:
        copy.wait()


def add_ladder(amp, integrals, old):
    parts = Z_HI * Y // 2
    rows, columns = old.shape
    vmem = pl.BlockSpec(memory_space=pltpu.VMEM)
    return pl.pallas_call(
        ladder_kernel,
        out_shape=jax.ShapeDtypeStruct(old.shape, old.dtype),
        in_specs=[vmem, vmem, vmem],
        out_specs=pl.BlockSpec(memory_space=pl.ANY),
        scratch_shapes=[
            pltpu.VMEM((parts, rows, columns // parts), jnp.float32),
            pltpu.SemaphoreType.DMA((parts,)),
        ],
        compiler_params=pltpu.CompilerParams(vmem_limit_bytes=32 * 1024 * 1024),
        cost_estimate=pl.CostEstimate(
            flops=2 * 256 * rows * columns, bytes_accessed=8 * rows * columns, transcendentals=0
        ),
    )(amp, integrals, old)


def per_device(amplitudes, integrals, old_residual):
    mine = integrals.T
    other = lax.ppermute(mine, "z_hi", [(0, 1), (1, 0)])
    amp_full = spread(amplitudes.T, ROW, Z_LO * CORES)
    low = lax.axis_index("z_hi") == 0
    both = jnp.stack([jnp.where(low, mine, other), jnp.where(low, other, mine)])
    integral_full = spread(both, PLANE, Y * X)
    return add_ladder(amp_full, integral_full, old_residual)


def solution(mesh):
    devices = mesh.devices.reshape(Z_LO, CORES, Z_HI, Y, X)
    fine = Mesh(devices, ROW + COL + ("x",))
    in_specs = (P(COL + ("x",), ROW), P(ROW + COL, "x"), P(COL + ("x",), ROW))
    out_specs = P(COL + ("x",), ROW)
    return jax.shard_map(
        per_device, mesh=fine, in_specs=in_specs, out_specs=out_specs, check_vma=False
    )
```

```python
import jax
import jax.numpy as jnp
from jax import lax
from jax.experimental import pallas as pl
from jax.experimental.pallas import tpu as pltpu
from jax.sharding import Mesh, PartitionSpec as P

Z_LO, CORES, Z_HI, Y, X = 8, 2, 2, 4, 4
ROW = ("z_lo", "core")
COL = ("z_hi", "y")
PLANE = ("y", "x")


def spread(block, axes, count):
    return lax.all_to_all(jnp.broadcast_to(block[None], (count,) + block.shape), axes, 0, 0)


def ladder_kernel(amp_ref, int_ref, old_ref, new_ref, held, sems):
    rows, width = held.shape[1:]
    amp = amp_ref[...].reshape(-1, rows)
    copies = []
    for part in range(held.shape[0]):
        half, pair = divmod(part, Y // 2)
        panels = []
        for y in (2 * pair, 2 * pair + 1):
            panel = int_ref[y * X:(y + 1) * X, half]
            panels.append(panel.reshape(-1, panel.shape[-1]))
        product = lax.dot_general(
            amp,
            jnp.concatenate(panels, axis=1),
            (((0,), (0,)), ((), ())),
            preferred_element_type=jnp.float32,
        )
        columns = pl.ds(part * width, width)
        held[part] = old_ref[:, columns] + product
        copy = pltpu.make_async_copy(held.at[part], new_ref.at[:, columns], sems.at[part])
        copy.start()
        copies.append(copy)
    for copy in copies:
        copy.wait()


def add_ladder(amp, integrals, old):
    parts = Z_HI * Y // 2
    rows, columns = old.shape
    vmem = pl.BlockSpec(memory_space=pltpu.VMEM)
    return pl.pallas_call(
        ladder_kernel,
        out_shape=jax.ShapeDtypeStruct(old.shape, old.dtype),
        in_specs=[vmem, vmem, vmem],
        out_specs=pl.BlockSpec(memory_space=pl.ANY),
        scratch_shapes=[
            pltpu.VMEM((parts, rows, columns // parts), jnp.float32),
            pltpu.SemaphoreType.DMA((parts,)),
        ],
        compiler_params=pltpu.CompilerParams(vmem_limit_bytes=32 * 1024 * 1024),
        cost_estimate=pl.CostEstimate(
            flops=2 * 256 * rows * columns, bytes_accessed=8 * rows * columns, transcendentals=0
        ),
    )(amp, integrals, old)


def per_device(amplitudes, integrals, old_residual):
    mine = integrals.T
    amp_full = spread(amplitudes.T, ROW, Z_LO * CORES)
    both = lax.all_gather(mine, "z_hi")
    integral_full = spread(both, PLANE, Y * X)
    return add_ladder(amp_full, integral_full, old_residual)


def solution(mesh):
    devices = mesh.devices.reshape(Z_LO, CORES, Z_HI, Y, X)
    fine = Mesh(devices, ROW + COL + ("x",))
    in_specs = (P(COL + ("x",), ROW), P(ROW + COL, "x"), P(COL + ("x",), ROW))
    out_specs = P(COL + ("x",), ROW)
    return jax.shard_map(
        per_device, mesh=fine, in_specs=in_specs, out_specs=out_specs, check_vma=False
    )
```

```python
import jax
import jax.numpy as jnp
from jax import lax
from jax.experimental import pallas as pl
from jax.experimental.pallas import tpu as pltpu
from jax.sharding import Mesh, PartitionSpec as P

Z_LO, CORES, Z_HI, Y, X = 8, 2, 2, 4, 4
ROW = ("z_lo", "core")
COL = ("z_hi", "y")
PLANE = ("y", "x")
Z_ORDER = (5, 6, 7, 4, 3, 2, 1, 0)
PLANE_ORDER = tuple((10 + i) % (Y * X) for i in range(Y * X))


def spread(block, axes, order):
    copies = jnp.broadcast_to(block[None], (len(order),) + block.shape)
    return lax.all_to_all(copies, axes, 0, 0, axis_index_groups=[list(order)])


def ladder_kernel(amp_ref, int_ref, old_ref, new_ref, held, sems):
    rows, width = held.shape[1:]
    amp = jnp.concatenate([amp_ref[Z_ORDER.index(z), c] for z in range(Z_LO) for c in range(CORES)])
    copies = []
    for part in range(held.shape[0]):
        half, pair = divmod(part, Y // 2)
        panels = []
        for y in (2 * pair, 2 * pair + 1):
            panels.append(jnp.concatenate([int_ref[PLANE_ORDER.index(y * X + x), half] for x in range(X)]))
        product = lax.dot_general(
            amp,
            jnp.concatenate(panels, axis=1),
            (((0,), (0,)), ((), ())),
            preferred_element_type=jnp.float32,
        )
        columns = pl.ds(part * width, width)
        held[part] = old_ref[:, columns] + product
        copy = pltpu.make_async_copy(held.at[part], new_ref.at[:, columns], sems.at[part])
        copy.start()
        copies.append(copy)
    for copy in copies:
        copy.wait()


def add_ladder(amp, integrals, old):
    parts = Z_HI * Y // 2
    rows, columns = old.shape
    vmem = pl.BlockSpec(memory_space=pltpu.VMEM)
    return pl.pallas_call(
        ladder_kernel,
        out_shape=jax.ShapeDtypeStruct(old.shape, old.dtype),
        in_specs=[vmem, vmem, vmem],
        out_specs=pl.BlockSpec(memory_space=pl.ANY),
        scratch_shapes=[
            pltpu.VMEM((parts, rows, columns // parts), jnp.float32),
            pltpu.SemaphoreType.DMA((parts,)),
        ],
        compiler_params=pltpu.CompilerParams(vmem_limit_bytes=32 * 1024 * 1024),
        cost_estimate=pl.CostEstimate(
            flops=2 * 256 * rows * columns, bytes_accessed=8 * rows * columns, transcendentals=0
        ),
    )(amp, integrals, old)


def per_device(amplitudes, integrals, old_residual):
    low = lax.axis_index("z_hi") == 0
    mine, amp = integrals.T, amplitudes.T
    down = lax.ppermute(mine, "z_hi", [(1, 0)])
    near = lax.cond(
        low,
        lambda a: spread(a, "z_lo", Z_ORDER),
        lambda a: jnp.zeros((Z_LO,) + a.shape, a.dtype),
        amp,
    )
    again, near = lax.optimization_barrier((mine, near))
    up = lax.ppermute(again, "z_hi", [(0, 1)])
    near = lax.cond(low, lambda a, n: n, lambda a, n: spread(a, "z_lo", Z_ORDER), amp, near)
    amp_full = lax.all_gather(near, "core", axis=1)
    both = jnp.stack([jnp.where(low, mine, up), jnp.where(low, down, mine)])
    integral_full = spread(both, PLANE, PLANE_ORDER)
    return add_ladder(amp_full, integral_full, old_residual)


def solution(mesh):
    devices = mesh.devices.reshape(Z_LO, CORES, Z_HI, Y, X)
    fine = Mesh(devices, ROW + COL + ("x",))
    in_specs = (P(COL + ("x",), ROW), P(ROW + COL, "x"), P(COL + ("x",), ROW))
    out_specs = P(COL + ("x",), ROW)
    return jax.shard_map(
        per_device, mesh=fine, in_specs=in_specs, out_specs=out_specs, check_vma=False
    )
```

```python
import jax
import jax.numpy as jnp
from jax import lax
from jax.experimental import pallas as pl
from jax.experimental.pallas import tpu as pltpu
from jax.sharding import Mesh, PartitionSpec as P

Z_LO, CORES, Z_HI, Y, X = 8, 2, 2, 4, 4
ROW = ("z_lo", "core")
COL = ("z_hi", "y")
PLANE = ("y", "x")
Z_ORDER = (6, 7, 5, 4, 3, 2, 1, 0)
PLANE_ORDER = tuple((10 + i) % (Y * X) for i in range(Y * X))


def spread(block, axes, order):
    copies = jnp.broadcast_to(block[None], (len(order),) + block.shape)
    return lax.all_to_all(copies, axes, 0, 0, axis_index_groups=[list(order)])


def ladder_kernel(amp_ref, int_ref, old_ref, new_ref, held, sems):
    rows, width = held.shape[1:]
    amp = jnp.concatenate([amp_ref[Z_ORDER.index(z), c] for z in range(Z_LO) for c in range(CORES)])
    copies = []
    for part in range(held.shape[0]):
        half, pair = divmod(part, Y // 2)
        panels = []
        for y in (2 * pair, 2 * pair + 1):
            panels.append(jnp.concatenate([int_ref[PLANE_ORDER.index(y * X + x), half] for x in range(X)]))
        product = lax.dot_general(
            amp,
            jnp.concatenate(panels, axis=1),
            (((0,), (0,)), ((), ())),
            preferred_element_type=jnp.float32,
        )
        columns = pl.ds(part * width, width)
        held[part] = old_ref[:, columns] + product
        copy = pltpu.make_async_copy(held.at[part], new_ref.at[:, columns], sems.at[part])
        copy.start()
        copies.append(copy)
    for copy in copies:
        copy.wait()


def add_ladder(amp, integrals, old):
    parts = Z_HI * Y // 2
    rows, columns = old.shape
    vmem = pl.BlockSpec(memory_space=pltpu.VMEM)
    return pl.pallas_call(
        ladder_kernel,
        out_shape=jax.ShapeDtypeStruct(old.shape, old.dtype),
        in_specs=[vmem, vmem, vmem],
        out_specs=pl.BlockSpec(memory_space=pl.ANY),
        scratch_shapes=[
            pltpu.VMEM((parts, rows, columns // parts), jnp.float32),
            pltpu.SemaphoreType.DMA((parts,)),
        ],
        compiler_params=pltpu.CompilerParams(vmem_limit_bytes=32 * 1024 * 1024),
        cost_estimate=pl.CostEstimate(
            flops=2 * 256 * rows * columns, bytes_accessed=8 * rows * columns, transcendentals=0
        ),
    )(amp, integrals, old)


def per_device(amplitudes, integrals, old_residual):
    low = lax.axis_index("z_hi") == 0
    mine, amp = integrals.T, amplitudes.T
    down = lax.ppermute(mine, "z_hi", [(1, 0)])
    near = lax.cond(
        low,
        lambda a: spread(a, "z_lo", Z_ORDER),
        lambda a: jnp.zeros((Z_LO,) + a.shape, a.dtype),
        amp,
    )
    again, near = lax.optimization_barrier((mine, near))
    up = lax.ppermute(again, "z_hi", [(0, 1)])
    near = lax.cond(low, lambda a, n: n, lambda a, n: spread(a, "z_lo", Z_ORDER), amp, near)
    amp_full = lax.all_gather(near, "core", axis=1)
    both = jnp.stack([jnp.where(low, mine, up), jnp.where(low, down, mine)])
    integral_full = spread(both, PLANE, PLANE_ORDER)
    return add_ladder(amp_full, integral_full, old_residual)


def solution(mesh):
    devices = mesh.devices.reshape(Z_LO, CORES, Z_HI, Y, X)
    fine = Mesh(devices, ROW + COL + ("x",))
    in_specs = (P(COL + ("x",), ROW), P(ROW + COL, "x"), P(COL + ("x",), ROW))
    out_specs = P(COL + ("x",), ROW)
    return jax.shard_map(
        per_device, mesh=fine, in_specs=in_specs, out_specs=out_specs, check_vma=False
    )
```

```python
import jax
import jax.numpy as jnp
from jax import lax
from jax.experimental import pallas as pl
from jax.experimental.pallas import tpu as pltpu
from jax.sharding import Mesh, PartitionSpec as P

Z_LO, CORES, Z_HI, Y, X = 8, 2, 2, 4, 4
ROW = ("z_lo", "core")
COL = ("z_hi", "y")
PLANE = ("y", "x")
Z_ORDER = (6, 7, 5, 4, 3, 2, 1, 0)
PLANE_ORDER = tuple((10 + i) % (Y * X) for i in range(Y * X))


def spread(block, axes, order):
    copies = jnp.broadcast_to(block[None], (len(order),) + block.shape)
    return lax.all_to_all(copies, axes, 0, 0, axis_index_groups=[list(order)])


def ladder_kernel(amp_ref, int_ref, old_ref, new_ref, held, sems):
    rows, width = held.shape[1:]
    amp = jnp.concatenate([amp_ref[Z_ORDER.index(z), c] for z in range(Z_LO) for c in range(CORES)])
    copies = []
    for part in range(held.shape[0]):
        half, pair = divmod(part, Y // 2)
        panels = []
        for y in (2 * pair, 2 * pair + 1):
            panels.append(jnp.concatenate([int_ref[PLANE_ORDER.index(y * X + x), half] for x in range(X)]))
        product = lax.dot_general(
            amp,
            jnp.concatenate(panels, axis=1),
            (((0,), (0,)), ((), ())),
            preferred_element_type=jnp.float32,
        )
        columns = pl.ds(part * width, width)
        held[part] = old_ref[:, columns] + product
        copy = pltpu.make_async_copy(held.at[part], new_ref.at[:, columns], sems.at[part])
        copy.start()
        copies.append(copy)
    for copy in copies:
        copy.wait()


def add_ladder(amp, integrals, old):
    parts = Z_HI * Y // 2
    rows, columns = old.shape
    vmem = pl.BlockSpec(memory_space=pltpu.VMEM)
    return pl.pallas_call(
        ladder_kernel,
        out_shape=jax.ShapeDtypeStruct(old.shape, old.dtype),
        in_specs=[vmem, vmem, vmem],
        out_specs=pl.BlockSpec(memory_space=pl.ANY),
        scratch_shapes=[
            pltpu.VMEM((parts, rows, columns // parts), jnp.float32),
            pltpu.SemaphoreType.DMA((parts,)),
        ],
        compiler_params=pltpu.CompilerParams(vmem_limit_bytes=32 * 1024 * 1024),
        cost_estimate=pl.CostEstimate(
            flops=2 * 256 * rows * columns, bytes_accessed=8 * rows * columns, transcendentals=0
        ),
    )(amp, integrals, old)


def high_spread(amp):
    order = (Z_ORDER[2], Z_ORDER[0], Z_ORDER[1]) + Z_ORDER[3:]
    got = spread(amp, "z_lo", order)
    return jnp.concatenate([got[1:3], got[:1], got[3:]])


def per_device(amplitudes, integrals, old_residual):
    low = lax.axis_index("z_hi") == 0
    mine, amp = integrals.T, amplitudes.T
    down = lax.ppermute(mine, "z_hi", [(1, 0)])
    near = lax.cond(
        low,
        lambda a: spread(a, "z_lo", Z_ORDER),
        lambda a: jnp.zeros((Z_LO,) + a.shape, a.dtype),
        amp,
    )
    again, near = lax.optimization_barrier((mine, near))
    up = lax.ppermute(again, "z_hi", [(0, 1)])
    near = lax.cond(low, lambda a, n: n, lambda a, n: high_spread(a), amp, near)
    amp_full = lax.all_gather(near, "core", axis=1)
    slots = jnp.broadcast_to(mine[None, None], (Y * X, Z_HI) + mine.shape)
    slots = lax.optimization_barrier(slots)
    other = jnp.where(low, down, up)
    other = jnp.broadcast_to(other[None, None], (Y * X, 1) + mine.shape)
    slots = lax.dynamic_update_slice(slots, other, (0, jnp.where(low, 1, 0), 0, 0))
    integral_full = lax.all_to_all(slots, PLANE, 0, 0, axis_index_groups=[list(PLANE_ORDER)])
    return add_ladder(amp_full, integral_full, old_residual)


def solution(mesh):
    devices = mesh.devices.reshape(Z_LO, CORES, Z_HI, Y, X)
    fine = Mesh(devices, ROW + COL + ("x",))
    in_specs = (P(COL + ("x",), ROW), P(ROW + COL, "x"), P(COL + ("x",), ROW))
    out_specs = P(COL + ("x",), ROW)
    return jax.shard_map(
        per_device, mesh=fine, in_specs=in_specs, out_specs=out_specs, check_vma=False
    )
```

```python
import jax
import jax.numpy as jnp
from jax import lax
from jax.experimental import pallas as pl
from jax.experimental.pallas import tpu as pltpu
from jax.sharding import Mesh, PartitionSpec as P

Z_LO, CORES, Z_HI, Y, X = 8, 2, 2, 4, 4
ROW = ("z_lo", "core")
COL = ("z_hi", "y")
PLANE = ("y", "x")
Z_ORDER = (6, 7, 5, 4, 3, 2, 1, 0)
PLANE_ORDER = tuple((10 + i) % (Y * X) for i in range(Y * X))


def spread(block, axes, order):
    copies = jnp.broadcast_to(block[None], (len(order),) + block.shape)
    return lax.all_to_all(copies, axes, 0, 0, axis_index_groups=[list(order)])


def ladder_kernel(amp_ref, int_ref, old_ref, new_ref, held, sems):
    rows, width = held.shape[1:]
    amp = jnp.concatenate([amp_ref[Z_ORDER.index(z), c] for z in range(Z_LO) for c in range(CORES)])
    copies = []
    for part in range(held.shape[0]):
        half, pair = divmod(part, Y // 2)
        panels = []
        for y in (2 * pair, 2 * pair + 1):
            panels.append(jnp.concatenate([int_ref[PLANE_ORDER.index(y * X + x), half] for x in range(X)]))
        product = lax.dot_general(
            amp,
            jnp.concatenate(panels, axis=1),
            (((0,), (0,)), ((), ())),
            preferred_element_type=jnp.float32,
        )
        columns = pl.ds(part * width, width)
        held[part] = old_ref[:, columns] + product
        copy = pltpu.make_async_copy(held.at[part], new_ref.at[:, columns], sems.at[part])
        copy.start()
        copies.append(copy)
    for copy in copies:
        copy.wait()


def add_ladder(amp, integrals, old):
    parts = Z_HI * Y // 2
    rows, columns = old.shape
    vmem = pl.BlockSpec(memory_space=pltpu.VMEM)
    return pl.pallas_call(
        ladder_kernel,
        out_shape=jax.ShapeDtypeStruct(old.shape, old.dtype),
        in_specs=[vmem, vmem, vmem],
        out_specs=pl.BlockSpec(memory_space=pl.ANY),
        scratch_shapes=[
            pltpu.VMEM((parts, rows, columns // parts), jnp.float32),
            pltpu.SemaphoreType.DMA((parts,)),
        ],
        compiler_params=pltpu.CompilerParams(vmem_limit_bytes=32 * 1024 * 1024),
        cost_estimate=pl.CostEstimate(
            flops=2 * 256 * rows * columns, bytes_accessed=8 * rows * columns, transcendentals=0
        ),
    )(amp, integrals, old)


def high_spread(amp):
    order = (Z_ORDER[2], Z_ORDER[0], Z_ORDER[1]) + Z_ORDER[3:]
    got = spread(amp, "z_lo", order)
    return jnp.concatenate([got[1:3], got[:1], got[3:]])


def per_device(amplitudes, integrals, old_residual):
    low = lax.axis_index("z_hi") == 0
    mine, amp = integrals.T, amplitudes.T
    down = lax.ppermute(mine, "z_hi", [(1, 0)])
    near = lax.cond(
        low,
        lambda a: spread(a, "z_lo", Z_ORDER),
        lambda a: jnp.zeros((Z_LO,) + a.shape, a.dtype),
        amp,
    )
    again, near = lax.optimization_barrier((mine, near))
    up = lax.ppermute(again, "z_hi", [(0, 1)])
    def filled(block):
        return jnp.broadcast_to(block[None, None], (Y * X, Z_HI) + block.shape)

    near, slots = lax.cond(
        low,
        lambda a, m, n: (n, filled(m)),
        lambda a, m, n: (high_spread(a), filled(m)),
        amp,
        mine,
        near,
    )
    amp_full = lax.all_gather(near, "core", axis=1)
    other = jnp.where(low, down, up)
    other = jnp.broadcast_to(other[None, None], (Y * X, 1) + mine.shape)
    slots = lax.dynamic_update_slice(slots, other, (0, jnp.where(low, 1, 0), 0, 0))
    integral_full = lax.all_to_all(slots, PLANE, 0, 0, axis_index_groups=[list(PLANE_ORDER)])
    return add_ladder(amp_full, integral_full, old_residual)


def solution(mesh):
    devices = mesh.devices.reshape(Z_LO, CORES, Z_HI, Y, X)
    fine = Mesh(devices, ROW + COL + ("x",))
    in_specs = (P(COL + ("x",), ROW), P(ROW + COL, "x"), P(COL + ("x",), ROW))
    out_specs = P(COL + ("x",), ROW)
    return jax.shard_map(
        per_device, mesh=fine, in_specs=in_specs, out_specs=out_specs, check_vma=False
    )
```

```python
import jax
import jax.numpy as jnp
from jax import lax
from jax.experimental import pallas as pl
from jax.experimental.pallas import tpu as pltpu
from jax.sharding import Mesh, PartitionSpec as P

Z_LO, CORES, Z_HI, Y, X = 8, 2, 2, 4, 4
ROW = ("z_lo", "core")
COL = ("z_hi", "y")
PLANE = ("y", "x")
Z_ORDER = (5, 6, 7, 4, 3, 2, 1, 0)
PLANE_ORDER = tuple((10 + i) % (Y * X) for i in range(Y * X))


def spread(block, axes, order):
    copies = jnp.broadcast_to(block[None], (len(order),) + block.shape)
    return lax.all_to_all(copies, axes, 0, 0, axis_index_groups=[list(order)])


def ladder_kernel(amp_ref, int_ref, old_ref, new_ref, held, sems):
    rows, width = held.shape[1:]
    amp = jnp.concatenate([amp_ref[Z_ORDER.index(z), c] for z in range(Z_LO) for c in range(CORES)])
    copies = []
    for part in range(held.shape[0]):
        half, pair = divmod(part, Y // 2)
        panels = []
        for y in (2 * pair, 2 * pair + 1):
            panels.append(jnp.concatenate([int_ref[PLANE_ORDER.index(y * X + x), half] for x in range(X)]))
        product = lax.dot_general(
            amp,
            jnp.concatenate(panels, axis=1),
            (((0,), (0,)), ((), ())),
            preferred_element_type=jnp.float32,
        )
        columns = pl.ds(part * width, width)
        held[part] = old_ref[:, columns] + product
        copy = pltpu.make_async_copy(held.at[part], new_ref.at[:, columns], sems.at[part])
        copy.start()
        copies.append(copy)
    for copy in copies:
        copy.wait()


def add_ladder(amp, integrals, old):
    parts = Z_HI * Y // 2
    rows, columns = old.shape
    vmem = pl.BlockSpec(memory_space=pltpu.VMEM)
    return pl.pallas_call(
        ladder_kernel,
        out_shape=jax.ShapeDtypeStruct(old.shape, old.dtype),
        in_specs=[vmem, vmem, vmem],
        out_specs=pl.BlockSpec(memory_space=pl.ANY),
        scratch_shapes=[
            pltpu.VMEM((parts, rows, columns // parts), jnp.float32),
            pltpu.SemaphoreType.DMA((parts,)),
        ],
        compiler_params=pltpu.CompilerParams(vmem_limit_bytes=32 * 1024 * 1024),
        cost_estimate=pl.CostEstimate(
            flops=2 * 256 * rows * columns, bytes_accessed=8 * rows * columns, transcendentals=0
        ),
    )(amp, integrals, old)


def per_device(amplitudes, integrals, old_residual):
    low = lax.axis_index("z_hi") == 0
    mine, amp = integrals.T, amplitudes.T
    down = lax.ppermute(mine, "z_hi", [(1, 0)])
    near = lax.cond(
        low,
        lambda a: spread(a, "z_lo", Z_ORDER),
        lambda a: jnp.zeros((Z_LO,) + a.shape, a.dtype),
        amp,
    )
    again, near = lax.optimization_barrier((mine, near))
    up = lax.ppermute(again, "z_hi", [(0, 1)])
    near = lax.cond(low, lambda a, n: n, lambda a, n: spread(a, "z_lo", Z_ORDER), amp, near)
    amp_full = lax.all_gather(near, "core", axis=1)
    slots = jnp.broadcast_to(mine[None, None], (Y * X, Z_HI) + mine.shape)
    slots = lax.optimization_barrier(slots)
    other = jnp.where(low, down, up)
    other = jnp.broadcast_to(other[None, None], (Y * X, 1) + mine.shape)
    slots = lax.dynamic_update_slice(slots, other, (0, jnp.where(low, 1, 0), 0, 0))
    integral_full = lax.all_to_all(slots, PLANE, 0, 0, axis_index_groups=[list(PLANE_ORDER)])
    return add_ladder(amp_full, integral_full, old_residual)


def solution(mesh):
    devices = mesh.devices.reshape(Z_LO, CORES, Z_HI, Y, X)
    fine = Mesh(devices, ROW + COL + ("x",))
    in_specs = (P(COL + ("x",), ROW), P(ROW + COL, "x"), P(COL + ("x",), ROW))
    out_specs = P(COL + ("x",), ROW)
    return jax.shard_map(
        per_device, mesh=fine, in_specs=in_specs, out_specs=out_specs, check_vma=False
    )
```
